32 devices in a mesh: dp: 8 (over y, x, core), seq: 4 (over z).
Axes of the slice: x: 2, y: 2, z: 4, core: 2. Of those that a mesh axis runs over, the one named last changes fastest.
Arguments:
- qkv: bfloat16 [3, 8, 2, 512, 3072], P(None, 'dp', None, 'seq'), may hold values from -18 to 18
- cotangent: bfloat16 [8, 2, 512, 3072], P('dp', None, 'seq'), may hold values from -6 to 6
- lengths: int32 [8, 2], replicated, may hold values from 0 to 512, as said below
- target_group: int32 [8, 2], replicated, may hold values from 0 to 7, as said below
- target_slot: int32 [8, 2], replicated, may hold values from 0 to 1, as said below
Outputs:
- attended: bfloat16 [8, 2, 512, 3072], P('dp', None, 'seq')
- grad_qkv: bfloat16 [3, 8, 2, 512, 3072], P(None, 'dp', None, 'seq')
The draws below stay inside these ranges and needn't reach their ends.
Inputs may be any that keep to these rules, and one draw needn't show every extreme that they name: Each group holds 0 to 2 clips; an empty slot has length 0, a clip has 128 to 512 tokens, and some clip has exactly 512. A move lowers the larger of the two groups' sums of squared clip lengths. `target_group`: A clip stays in its group or moves to the group one below or one above; a group sends at most one clip to each neighbour and at most one clip arrives in a group; a group that sends receives nothing; group 0 sends one clip to group 1 and the last group one to the group below it; empty slots name their own group. `target_slot`: A clip that stays keeps its slot; a moving clip lands in a slot of its destination that holds no clip before the moves; empty slots name their own slot.
All inputs are finite; a program needn't handle non-finite values.
Results may differ from the reference program's by a relative error of at most 0.0049.
Values may be sent and summed in bfloat16 or wider, within the bound.
A program may use at most 128 MiB of HBM per device.

```python
import jax
import jax.numpy as jnp
from jax import lax

HEADS = 24
HEAD = 128
CAP = 512
SLOTS = 2
GROUPS = 8


def clip_plan(key):
    subkeys = jax.random.split(key, 5)
    group_numbers = jnp.arange(GROUPS, dtype=jnp.int32)
    level = jax.random.randint(subkeys[0], (GROUPS,), 0, 8)
    clips = jnp.where(level < 1, 0, jnp.where(level < 4, 1, 2)).astype(jnp.int32)
    clips = clips.at[0].set(2).at[1].set(1).at[GROUPS - 3].set(1).at[GROUPS - 2].set(1).at[GROUPS - 1].set(2)
    coin_flips = jax.random.randint(subkeys[1], (GROUPS,), 0, 4)
    coin_flips = coin_flips.at[0].set(1).at[GROUPS - 1].set(3)
    clips_above = jnp.concatenate([clips[1:], jnp.zeros((1,), jnp.int32)])
    clips_below = jnp.concatenate([jnp.zeros((1,), jnp.int32), clips[:-1]])

    def advance(carry, inputs):
        taken_below, taken_here = carry
        own_clips, upper_clips, lower_clips, coin_value, group_number = inputs
        can_up = (own_clips == 2) & (group_number + 1 < GROUPS) & (upper_clips == 1)
        can_down = (own_clips == 2) & (group_number > 0) & (lower_clips == 1) & (taken_below == 0)
        prefer_up = jnp.where(can_up, 1, jnp.where(can_down, -1, 0))
        prefer_down = jnp.where(can_down, -1, jnp.where(can_up, 1, 0))
        direction = jnp.where(coin_value == 3, prefer_down, prefer_up).astype(jnp.int32)
        return ((taken_here, (direction == 1).astype(jnp.int32)), direction)
    initial = (jnp.zeros((), jnp.int32), jnp.zeros((), jnp.int32))
    _, directions = lax.scan(advance, initial, (clips, clips_above, clips_below, coin_flips, group_numbers))
    single = jax.random.randint(subkeys[3], (GROUPS,), 0, SLOTS)
    slot_numbers = jnp.arange(SLOTS, dtype=jnp.int32)[None, :]
    occupied = jnp.where(clips[:, None] == 2, True, jnp.where(clips[:, None] == 1, slot_numbers == single[:, None], False))
    long_sizes = jax.random.randint(subkeys[4], (GROUPS, SLOTS), CAP // 2, CAP + 1)
    short_sizes = jax.random.randint(subkeys[2], (GROUPS, SLOTS), CAP // 4, CAP // 2)
    sizes = jnp.where(clips[:, None] == 2, long_sizes, short_sizes)
    sizes = jnp.where(occupied, sizes, 0)
    sizes = sizes.at[0, 0].set(CAP).astype(jnp.int32)
    moving_slot = jnp.where(sizes[:, 1] < sizes[:, 0], 1, 0).astype(jnp.int32)
    moving = occupied & (clips[:, None] == 2) & (slot_numbers == moving_slot[:, None]) & (directions[:, None] != 0)
    destination = group_numbers + directions
    clamped = jnp.clip(destination, 0, GROUPS - 1)
    free_slot = SLOTS - 1 - single
    target_group = jnp.where(moving, destination[:, None], jnp.broadcast_to(group_numbers[:, None], (GROUPS, SLOTS)))
    target_slot = jnp.where(moving, free_slot[clamped][:, None], jnp.broadcast_to(slot_numbers, (GROUPS, SLOTS)))
    return (sizes, target_group.astype(jnp.int32), target_slot.astype(jnp.int32))


def draw_lengths(key, part):
    drawn_plan = clip_plan(key)
    return drawn_plan[0]


def draw_target_group(key, part):
    drawn_plan = clip_plan(key)
    return drawn_plan[1]


def draw_target_slot(key, part):
    drawn_plan = clip_plan(key)
    return drawn_plan[2]


def draw_qkv(key, part):
    key = jax.random.fold_in(key, 7)
    subkeys = jax.random.split(key, 1)
    features = HEADS * HEAD
    extents = (3, GROUPS, SLOTS, CAP, features)
    array_scale = jnp.array([2.5, 1.0, 1.0], jnp.float32).reshape(3, 1, 1, 1, 1)
    values = jax.random.truncated_normal(subkeys[0], -6.0, 6.0, extents, jnp.float32) * array_scale
    return values.astype(jnp.bfloat16)


def level_of(own_key, shape, shards, low, top_value):
    loudness, own = 1.0, jax.random.fold_in(own_key, 6)
    for axis_at, blocks in shards:
        heights = jnp.exp(jax.random.uniform(jax.random.fold_in(own, axis_at), (blocks,), jnp.float32, low / len(shards), top_value / len(shards)))
        loudness = loudness * jnp.repeat(heights, shape[axis_at] // blocks).reshape([-1 if axis == axis_at else 1 for axis in range(len(shape))])
    return loudness


def scatter_about(stream_key, shape, spread, reach, cuts=(), kind=jnp.bfloat16):
    gain = level_of(stream_key, shape, cuts, -0.22, 0.18) if cuts else 1.0
    values = jax.random.normal(stream_key, shape, jnp.float32) * spread * gain
    return jnp.minimum(jnp.maximum(values, -reach), reach).astype(kind)


def setup_inputs(seed: int = 0) -> dict:
    key_of = jax.random.split(jax.random.key(seed), 6)
    return {
        "qkv": draw_qkv(jax.random.fold_in(key_of[5], 71), 0),
        "cotangent": scatter_about(key_of[1], (GROUPS, SLOTS, CAP, HEADS * HEAD), 1.0, 6.0, ((0, 8), (2, 4))),
        "lengths": draw_lengths(jax.random.fold_in(key_of[5], 71), 0),
        "target_group": draw_target_group(jax.random.fold_in(key_of[5], 71), 0),
        "target_slot": draw_target_slot(jax.random.fold_in(key_of[5], 71), 0),
    }


def clip_pass(packed, upstream, count):
    extent = packed.shape[1]
    features = packed.shape[2]
    head_count = features // HEAD
    factor = HEAD ** -0.5
    queries = packed[0].astype(jnp.float32).reshape(extent, head_count, HEAD)
    key_heads = packed[1].astype(jnp.float32).reshape(extent, head_count, HEAD)
    value_heads = packed[2].astype(jnp.float32).reshape(extent, head_count, HEAD)
    scores = jnp.einsum("qhd,khd->hqk", queries, key_heads) * factor
    position = jnp.arange(extent)
    scores = jnp.where(position[None, None, :] < count, scores, -1.0e30)
    largest = jnp.max(scores, axis=2, keepdims=True)
    exponent = jnp.exp(scores - largest)
    weights = exponent / jnp.sum(exponent, axis=2, keepdims=True)
    rounded = lax.optimization_barrier(weights.astype(jnp.bfloat16)).astype(jnp.float32)
    inside = (position < count)[:, None, None]
    output = jnp.einsum("hqk,khd->qhd", rounded, value_heads)
    output = jnp.where(inside, output, 0.0).astype(jnp.bfloat16).reshape(extent, features)
    grad_rows = jnp.where(inside, upstream.astype(jnp.float32).reshape(extent, head_count, HEAD), 0.0)
    grad_weights = jnp.einsum("qhd,khd->hqk", grad_rows, value_heads)
    inner_sum = jnp.sum(grad_weights * weights, axis=2, keepdims=True)
    score_grad = weights * (grad_weights - inner_sum)
    rounded_grad = lax.optimization_barrier(score_grad.astype(jnp.bfloat16)).astype(jnp.float32)
    grad_q = (jnp.einsum("hqk,khd->qhd", rounded_grad, key_heads) * factor).astype(jnp.bfloat16)
    grad_k = (jnp.einsum("hqk,qhd->khd", rounded_grad, queries) * factor).astype(jnp.bfloat16)
    grad_v = jnp.einsum("hqk,qhd->khd", rounded, grad_rows).astype(jnp.bfloat16)
    gradients = jnp.stack([grad_q, grad_k, grad_v]).reshape(3, extent, features)
    return output, gradients


def reference(qkv, cotangent, lengths, target_group, target_slot):
    groups = lengths.shape[0]
    slot_count = lengths.shape[1]
    extent = qkv.shape[3]
    features = qkv.shape[4]
    home_grad = cotangent[target_group, target_slot]
    flat_qkv = jnp.moveaxis(qkv, 0, 2).reshape(groups * slot_count, 3, extent, features)

    def per_clip(bundle):
        return clip_pass(bundle[0], bundle[1], bundle[2])

    outputs, gradients = lax.map(per_clip, (flat_qkv, home_grad.reshape(groups * slot_count, extent, features), lengths.reshape(-1)))
    attended = jnp.zeros((groups, slot_count, extent, features), jnp.float32)
    attended = attended.at[target_group.reshape(-1), target_slot.reshape(-1)].add(outputs.astype(jnp.float32))
    attended = attended.astype(jnp.bfloat16)
    grad_qkv = jnp.moveaxis(gradients.reshape(groups, slot_count, 3, extent, features), 2, 0)
    return attended, grad_qkv
```

```python
import functools

import jax
import jax.numpy as jnp
from jax import lax
from jax.experimental import pallas as pl
from jax.experimental.pallas import tpu as pltpu
from jax.sharding import PartitionSpec as P

HEAD = 128
FACTOR = HEAD**-0.5
LOG2E = 1.4426950408889634
NEGATIVE = -1e30


def table_row(table, number):
    return lax.dynamic_index_in_dim(table, number, 0, keepdims=False)


def shift_dp(block, distance):
    size = lax.axis_size("dp")
    route = [(i - distance, i) for i in range(size) if 0 <= i - distance < size]
    return lax.ppermute(block, "dp", route)


def invert(lengths, to_group, to_slot):
    groups, slot_count = lengths.shape
    group_numbers = jnp.arange(groups, dtype=jnp.int32)
    slot_numbers = jnp.arange(slot_count, dtype=jnp.int32)
    match = (
        (lengths > 0)[:, :, None, None]
        & (to_group[:, :, None, None] == group_numbers[None, None, :, None])
        & (to_slot[:, :, None, None] == slot_numbers[None, None, None, :])
    ).astype(jnp.int32)
    from_group = jnp.sum(match * group_numbers[:, None, None, None], axis=(0, 1))
    from_slot = jnp.sum(match * slot_numbers[None, :, None, None], axis=(0, 1))
    arrived = jnp.sum(match, axis=(0, 1))
    return from_group, from_slot, arrived > 0


def relocate(blocks, to_group, to_slot, occupied):
    groups, slot_count = to_group.shape
    current = lax.axis_index("dp")
    own_group = table_row(to_group, current)
    own_slot = table_row(to_slot, current)
    own_occupied = table_row(occupied, current)
    zero = jnp.zeros((), blocks.dtype)

    def pick(mask):
        return table_row(blocks, jnp.argmax(mask).astype(jnp.int32))

    from_below = shift_dp(pick(own_occupied & (own_group == current + 1)), 1)
    from_above = shift_dp(pick(own_occupied & (own_group == current - 1)), -1)

    def landing(other, slot):
        inside = (other >= 0) & (other < groups)
        other = jnp.clip(other, 0, groups - 1)
        return inside & jnp.any(
            table_row(occupied, other)
            & (table_row(to_group, other) == current)
            & (table_row(to_slot, other) == slot)
        )

    result = []
    for slot in range(slot_count):
        block = jnp.full(blocks.shape[1:], zero)
        for source in range(slot_count):
            stays = own_occupied[source] & (own_group[source] == current)
            block = jnp.where(stays & (own_slot[source] == slot), blocks[source], block)
        block = jnp.where(landing(current - 1, slot), from_below, block)
        block = jnp.where(landing(current + 1, slot), from_above, block)
        result.append(block)
    return result


def attention_kernel(parts, plan_ref, *refs):
    ins, outs = refs[:parts], refs[parts:]
    rows = ins[0].shape[1]
    extent = parts * rows
    count = plan_ref[parts]
    row_iota = lax.broadcasted_iota(jnp.int32, (rows, 1), 0)
    inside = jnp.concatenate([row_iota + plan_ref[d] < count for d in range(parts)], axis=0)

    def load(which):
        return jnp.concatenate([r[which] for r in ins], axis=0)

    q, k, v, g = load(0), load(1), load(2), load(3)
    g = jnp.where(inside, g, jnp.zeros((), g.dtype))
    nt = (((1,), (1,)), ((), ()))
    tn = (((0,), (0,)), ((), ()))
    nn = (((1,), (0,)), ((), ()))
    dot = functools.partial(lax.dot_general, preferred_element_type=jnp.float32)
    grad_k = grad_v = None
    out_rows, grad_q_rows = [], []
    step = min(256, extent)
    for start in range(0, extent, step):
        stop = min(start + step, extent)
        q_i, g_i = q[start:stop], g[start:stop]
        scores = jnp.where(inside, dot(k, q_i, nt), NEGATIVE)
        largest = jnp.max(scores, axis=0, keepdims=True)
        exponent = jnp.exp2((scores - largest) * (FACTOR * LOG2E))
        weights = exponent * (1.0 / jnp.sum(exponent, axis=0, keepdims=True))
        rounded = weights.astype(jnp.bfloat16)
        grad_weights = dot(v, g_i, nt)
        inner = jnp.sum(grad_weights * weights, axis=0, keepdims=True)
        score_grad = (weights * (grad_weights - inner)).astype(jnp.bfloat16)
        out_rows.append(dot(v, rounded, tn).T)
        grad_q_rows.append(dot(k, score_grad, tn).T)
        add_k = dot(score_grad, q_i, nn)
        add_v = dot(rounded, g_i, nn)
        grad_k = add_k if grad_k is None else grad_k + add_k
        grad_v = add_v if grad_v is None else grad_v + add_v
    out = jnp.where(inside, jnp.concatenate(out_rows, axis=0), 0.0).astype(jnp.bfloat16)
    grad_q = (jnp.concatenate(grad_q_rows, axis=0) * FACTOR).astype(jnp.bfloat16)
    grad_k = (grad_k * FACTOR).astype(jnp.bfloat16)
    grad_v = grad_v.astype(jnp.bfloat16)
    for d, ref in enumerate(outs):
        span = slice(d * rows, (d + 1) * rows)
        ref[0] = out[span]
        ref[1] = grad_q[span]
        ref[2] = grad_k[span]
        ref[3] = grad_v[span]


def attention(pieces, plan):
    parts = len(pieces)
    fields, rows, width = pieces[0].shape
    spec = pl.BlockSpec((fields, rows, HEAD), lambda h, plan: (0, 0, h))
    return pl.pallas_call(
        functools.partial(attention_kernel, parts),
        out_shape=[jax.ShapeDtypeStruct(p.shape, p.dtype) for p in pieces],
        grid_spec=pltpu.PrefetchScalarGridSpec(
            num_scalar_prefetch=1,
            grid=(width // HEAD,),
            in_specs=[spec] * parts,
            out_specs=[spec] * parts,
        ),
        compiler_params=pltpu.CompilerParams(vmem_limit_bytes=40 * 2**20),
    )(plan, *pieces)


def clip_runner(parts):
    def run(packed, upstream, count):
        rows, features = upstream.shape
        width = features // parts
        me = lax.axis_index("seq")
        takes_part = me < parts

        def rotate(block, distance):
            return lax.ppermute(
                block, "seq", [(i, (i + distance) % parts) for i in range(parts)]
            )

        def chunk(distance):
            at = lax.rem(me + distance, parts) * width
            return jnp.concatenate(
                [
                    lax.dynamic_slice_in_dim(packed, at, width, 2),
                    lax.dynamic_slice_in_dim(upstream, at, width, 1)[None],
                ],
                axis=0,
            )

        pieces = [chunk(0)] + [rotate(chunk(d), d) for d in range(1, parts)]
        starts = [
            jnp.where(takes_part, lax.rem(me - d + 2 * parts, parts), parts) * rows
            for d in range(parts)
        ]
        starts = [jnp.where(takes_part, s, parts * rows) for s in starts]
        plan = jnp.stack(starts + [count]).astype(jnp.int32)
        results = attention(pieces, plan)
        out = jnp.zeros((4, rows, features), jnp.bfloat16)
        for d in range(parts):
            block = results[d] if d == 0 else rotate(results[d], parts - d)
            at = lax.rem(me + d, parts) * width
            out = lax.dynamic_update_slice_in_dim(out, block, at, 2)
        return out

    return run


def skip_clip(packed, upstream, count):
    return jnp.zeros((4,) + upstream.shape, jnp.bfloat16)


def on_device(qkv, cotangent, lengths, target_group, target_slot):
    packed = qkv[:, 0]
    _, slot_count, rows, features = packed.shape
    heads = features // HEAD
    size = lax.axis_size("seq")
    current = lax.axis_index("dp")
    occupied = lengths > 0
    from_group, from_slot, arrived = invert(lengths, target_group, target_slot)
    home_grad = relocate(cotangent[0], from_group, from_slot, arrived)
    counts = table_row(lengths, current)
    choices = [p for p in range(1, size + 1) if heads % p == 0]
    branches = [skip_clip] + [clip_runner(p) for p in choices]
    results = []
    for slot in range(slot_count):
        count = counts[slot]
        which = (count > 0).astype(jnp.int32)
        for p in choices[:-1]:
            which = which + (count > p * rows).astype(jnp.int32)
        results.append(lax.switch(which, branches, packed[:, slot], home_grad[slot], count))
    outs = jnp.stack([r[0] for r in results])
    attended = relocate(outs, target_group, target_slot, occupied)
    grads = jnp.stack([r[1:] for r in results], axis=1)
    return jnp.stack(attended)[None], grads[:, None]


def solution(mesh):
    in_specs = (P(None, "dp", None, "seq", None), P("dp", None, "seq", None), P(), P(), P())
    out_specs = (P("dp", None, "seq", None), P(None, "dp", None, "seq", None))
    return jax.shard_map(
        on_device, mesh=mesh, in_specs=in_specs, out_specs=out_specs, check_vma=False
    )
```

```python
import functools

import jax
import jax.numpy as jnp
from jax import lax
from jax.experimental import pallas as pl
from jax.experimental.pallas import tpu as pltpu
from jax.sharding import PartitionSpec as P

HEAD = 128
FACTOR = HEAD**-0.5
LOG2E = 1.4426950408889634
NEGATIVE = -1e30


SMEM = pltpu.MemorySpace.SMEM
PICK_UP, PICK_DOWN, BRANCH = 0, 1, 2
SLOT, COUNT, SOURCE, OWN = 3, 5, 7, 9
SEND_UP, SEND_DOWN, PLACE = 11, 12, 13
PLAN = 16


def shift_dp(block, distance):
    size = lax.axis_size("dp")
    route = [(i - distance, i) for i in range(size) if 0 <= i - distance < size]
    return lax.ppermute(block, "dp", route)


def extents(size, heads):
    return [p for p in range(1, size + 1) if heads % p == 0 and 2 * p >= size]


def copies_of(pairs, sems):
    return [pltpu.make_async_copy(a, b, sems.at[i]) for i, (a, b) in enumerate(pairs)]


def plan_kernel(choices, rows, lengths, to_group, to_slot, cot, plan, up, down, sems):
    groups = lengths.shape[0]
    me = lax.axis_index("dp")

    def entry(group, slot):
        return lengths[group, slot] > 0, to_group[group, slot], to_slot[group, slot]

    pick_up = pick_down = send_up = send_down = jnp.int32(0)
    place = [jnp.int32(0), jnp.int32(0)]
    upper, lower = jnp.minimum(me + 1, groups - 1), jnp.maximum(me - 1, 0)
    ranks, sources, owns = [], [], []
    for slot in range(2):
        full, group, target = entry(upper, slot)
        arrives = full & (group == me) & (me + 1 < groups)
        pick_up = jnp.where(arrives, target, pick_up)
        place = [jnp.where(arrives & (target == t), 4, place[t]) for t in range(2)]
        full, group, target = entry(lower, slot)
        arrives = full & (group == me) & (me > 0)
        pick_down = jnp.where(arrives, target, pick_down)
        place = [jnp.where(arrives & (target == t), 3, place[t]) for t in range(2)]
        full, group, target = entry(me, slot)
        send_up = jnp.where(full & (group == me + 1), slot, send_up)
        send_down = jnp.where(full & (group == me - 1), slot, send_down)
        stays = full & (group == me)
        place = [jnp.where(stays & (target == t), 1 + slot, place[t]) for t in range(2)]
        sources.append(jnp.where(group == me + 1, 2, jnp.where(group == me - 1, 1, 0)))
        owns.append(target)
        count = lengths[me, slot]
        rank = jnp.where(count > 0, 1, 0)
        for p in choices[:-1]:
            rank = rank + jnp.where(count > p * rows, 1, 0)
        ranks.append(rank)
    swap = ranks[1] > ranks[0]
    first = jnp.where(swap, ranks[1], ranks[0])
    second = jnp.where(swap, ranks[0], ranks[1])
    plan[PICK_UP] = pick_up
    plan[PICK_DOWN] = pick_down
    plan[BRANCH] = first * (first + 1) // 2 + second
    for i in range(2):
        plan[SLOT + i] = jnp.where(swap, 1 - i, i)
        plan[COUNT + i] = jnp.where(swap, lengths[me, 1 - i], lengths[me, i])
        plan[SOURCE + i] = jnp.where(swap, sources[1 - i], sources[i])
        plan[OWN + i] = jnp.where(swap, owns[1 - i], owns[i])
        plan[PLACE + i] = place[i]
    plan[SEND_UP] = send_up
    plan[SEND_DOWN] = send_down
    plan[PLAN - 1] = 0
    moves = copies_of([(cot.at[pick_up], up), (cot.at[pick_down], down)], sems)
    for move in moves:
        move.start()
    for move in moves:
        move.wait()


def make_plan(choices, lengths, to_group, to_slot, cot):
    block = jax.ShapeDtypeStruct(cot.shape[1:], cot.dtype)
    return pl.pallas_call(
        functools.partial(plan_kernel, choices, cot.shape[1]),
        out_shape=[jax.ShapeDtypeStruct((PLAN,), jnp.int32), block, block],
        in_specs=[pl.BlockSpec(memory_space=SMEM)] * 3 + [pl.BlockSpec(memory_space=pl.ANY)],
        out_specs=[pl.BlockSpec(memory_space=SMEM)] + [pl.BlockSpec(memory_space=pl.ANY)] * 2,
        scratch_shapes=[pltpu.SemaphoreType.DMA((2,))],
    )(lengths, to_group, to_slot, cot)


def pick_kernel(plan, blocks, up, down, sems):
    moves = copies_of(
        [(blocks.at[plan[SEND_UP]], up), (blocks.at[plan[SEND_DOWN]], down)], sems
    )
    for move in moves:
        move.start()
    for move in moves:
        move.wait()


def pick_outputs(plan, blocks):
    block = jax.ShapeDtypeStruct(blocks.shape[1:], blocks.dtype)
    return pl.pallas_call(
        pick_kernel,
        out_shape=[block, block],
        in_specs=[pl.BlockSpec(memory_space=SMEM), pl.BlockSpec(memory_space=pl.ANY)],
        out_specs=[pl.BlockSpec(memory_space=pl.ANY)] * 2,
        scratch_shapes=[pltpu.SemaphoreType.DMA((2,))],
    )(plan, blocks)


def place_kernel(plan, blocks, below, above, out, zeros, sems):
    zeros[...] = jnp.zeros_like(zeros)
    for t in range(2):
        for code, source in enumerate([zeros, blocks.at[0], blocks.at[1], below, above]):

            @pl.when(plan[PLACE + t] == code)
            def _():
                pltpu.make_async_copy(source, out.at[t], sems.at[t]).start()

    for t in range(2):
        pltpu.make_async_copy(below, out.at[t], sems.at[t]).wait()


def place_outputs(plan, blocks, below, above):
    return pl.pallas_call(
        place_kernel,
        out_shape=jax.ShapeDtypeStruct(blocks.shape, blocks.dtype),
        in_specs=[pl.BlockSpec(memory_space=SMEM)] + [pl.BlockSpec(memory_space=pl.ANY)] * 3,
        out_specs=pl.BlockSpec(memory_space=pl.ANY),
        scratch_shapes=[
            pltpu.VMEM(blocks.shape[1:], blocks.dtype),
            pltpu.SemaphoreType.DMA((2,)),
        ],
    )(plan, blocks, below, above)


def pack_kernel(parts, clip, plan, qkv, cot, below, above, *refs):
    pieces, sems = refs[:parts], refs[parts]
    width = pieces[0].shape[2]
    me = lax.axis_index("seq")
    slot, source, own = plan[SLOT + clip], plan[SOURCE + clip], plan[OWN + clip]

    def columns(d):
        return pl.ds(pl.multiple_of(lax.rem(me + d, parts) * width, HEAD), width)

    moves = [
        pltpu.make_async_copy(
            qkv.at[:, slot, :, columns(d)], pieces[d].at[pl.ds(0, 3)], sems.at[d]
        )
        for d in range(parts)
    ]
    for move in moves:
        move.start()
    for code, block in enumerate([cot.at[own], below, above]):

        @pl.when(source == code)
        def _():
            for d in range(parts):
                pltpu.make_async_copy(
                    block.at[:, columns(d)], pieces[d].at[3], sems.at[parts + d]
                ).start()

    for move in moves:
        move.wait()
    for d in range(parts):
        pltpu.make_async_copy(
            below.at[:, columns(d)], pieces[d].at[3], sems.at[parts + d]
        ).wait()


def pack(parts, clip, plan, qkv, cot, below, above):
    rows, features = below.shape
    piece = jax.ShapeDtypeStruct((4, rows, features // parts), qkv.dtype)
    return pl.pallas_call(
        functools.partial(pack_kernel, parts, clip),
        out_shape=[piece] * parts,
        in_specs=[pl.BlockSpec(memory_space=SMEM)] + [pl.BlockSpec(memory_space=pl.ANY)] * 4,
        out_specs=[pl.BlockSpec(memory_space=pl.ANY)] * parts,
        scratch_shapes=[pltpu.SemaphoreType.DMA((2 * parts,))],
    )(plan, qkv, cot, below, above)


def assemble_kernel(parts, clip, plan, *refs):
    sems, zeros = refs[-1], refs[-2]
    outs, grads = refs[-4], refs[-3]
    slot = plan[SLOT + clip]
    me = lax.axis_index("seq")
    pairs = []
    if parts:
        width = refs[0].shape[2]
        for d in range(parts):
            columns = pl.ds(pl.multiple_of(lax.rem(me + d, parts) * width, HEAD), width)
            pairs.append((refs[d].at[0], outs.at[slot, :, columns]))
            pairs.append((refs[d].at[pl.ds(1, 3)], grads.at[:, slot, :, columns]))
    else:
        zeros[...] = jnp.zeros_like(zeros)
        pairs.append((zeros, outs.at[slot]))
        for i in range(3):
            pairs.append((zeros, grads.at[i, slot]))
    moves = copies_of(pairs, sems)
    for move in moves:
        move.start()
    for move in moves:
        move.wait()


def assemble(clip, plan, pieces, qkv, totals):
    parts = len(pieces)
    rows, features = qkv.shape[2:]
    any_space = pl.BlockSpec(memory_space=pl.ANY)
    operands = list(pieces) + list(totals)
    aliases = {1 + parts + i: i for i in range(len(totals))}
    return pl.pallas_call(
        functools.partial(assemble_kernel, parts, clip),
        out_shape=[
            jax.ShapeDtypeStruct(qkv.shape[1:], qkv.dtype),
            jax.ShapeDtypeStruct(qkv.shape, qkv.dtype),
        ],
        in_specs=[pl.BlockSpec(memory_space=SMEM)] + [any_space] * len(operands),
        out_specs=[any_space] * 2,
        scratch_shapes=[
            pltpu.VMEM((16, 128) if parts else (rows, features), qkv.dtype),
            pltpu.SemaphoreType.DMA((max(2 * parts, 4),)),
        ],
        input_output_aliases=aliases,
    )(plan, *operands)


def attention_kernel(parts, plan_ref, *refs):
    ins, outs = refs[:parts], refs[parts:]
    rows = ins[0].shape[1]
    extent = parts * rows
    count = plan_ref[parts]
    row_iota = lax.broadcasted_iota(jnp.int32, (rows, 1), 0)
    inside = jnp.concatenate([row_iota + plan_ref[d] < count for d in range(parts)], axis=0)

    def load(which):
        return jnp.concatenate([r[which] for r in ins], axis=0)

    q, k, v, g = load(0), load(1), load(2), load(3)
    g = jnp.where(inside, g, jnp.zeros((), g.dtype))
    nt = (((1,), (1,)), ((), ()))
    tn = (((0,), (0,)), ((), ()))
    nn = (((1,), (0,)), ((), ()))
    dot = functools.partial(lax.dot_general, preferred_element_type=jnp.float32)
    grad_k = grad_v = None
    out_rows, grad_q_rows = [], []
    step = min(256, extent)
    for start in range(0, extent, step):
        stop = min(start + step, extent)
        q_i, g_i = q[start:stop], g[start:stop]
        scores = jnp.where(inside, dot(k, q_i, nt), NEGATIVE)
        largest = jnp.max(scores, axis=0, keepdims=True)
        exponent = jnp.exp2((scores - largest) * (FACTOR * LOG2E))
        weights = exponent * (1.0 / jnp.sum(exponent, axis=0, keepdims=True))
        rounded = weights.astype(jnp.bfloat16)
        grad_weights = dot(v, g_i, nt)
        inner = jnp.sum(grad_weights * weights, axis=0, keepdims=True)
        score_grad = (weights * (grad_weights - inner)).astype(jnp.bfloat16)
        out_rows.append(dot(v, rounded, tn).T)
        grad_q_rows.append(dot(k, score_grad, tn).T)
        add_k = dot(score_grad, q_i, nn)
        add_v = dot(rounded, g_i, nn)
        grad_k = add_k if grad_k is None else grad_k + add_k
        grad_v = add_v if grad_v is None else grad_v + add_v
    out = jnp.where(inside, jnp.concatenate(out_rows, axis=0), 0.0).astype(jnp.bfloat16)
    grad_q = (jnp.concatenate(grad_q_rows, axis=0) * FACTOR).astype(jnp.bfloat16)
    grad_k = (grad_k * FACTOR).astype(jnp.bfloat16)
    grad_v = grad_v.astype(jnp.bfloat16)
    for d, ref in enumerate(outs):
        span = slice(d * rows, (d + 1) * rows)
        ref[0] = out[span]
        ref[1] = grad_q[span]
        ref[2] = grad_k[span]
        ref[3] = grad_v[span]


def attention(pieces, plan):
    parts = len(pieces)
    fields, rows, width = pieces[0].shape
    spec = pl.BlockSpec((fields, rows, HEAD), lambda h, plan: (0, 0, h))
    return pl.pallas_call(
        functools.partial(attention_kernel, parts),
        out_shape=[jax.ShapeDtypeStruct(p.shape, p.dtype) for p in pieces],
        grid_spec=pltpu.PrefetchScalarGridSpec(
            num_scalar_prefetch=1,
            grid=(width // HEAD,),
            in_specs=[spec] * parts,
            out_specs=[spec] * parts,
        ),
        compiler_params=pltpu.CompilerParams(vmem_limit_bytes=40 * 2**20),
        cost_estimate=pl.CostEstimate(
            flops=12 * (parts * rows) ** 2 * width,
            bytes_accessed=16 * parts * rows * width,
            transcendentals=(parts * rows) ** 2 * (width // HEAD),
        ),
    )(plan, *pieces)


def rotate(parts, block, distance):
    return lax.ppermute(block, "seq", [(i, (i + distance) % parts) for i in range(parts)])


def pair_runner(shares):
    def run(plan, qkv, cot, below, above):
        rows = below.shape[0]
        me = lax.axis_index("seq")
        arrived = []
        for clip, parts in enumerate(shares):
            if parts:
                pieces = pack(parts, clip, plan, qkv, cot, below, above)
                arrived.append(
                    [pieces[0]] + [rotate(parts, pieces[d], d) for d in range(1, parts)]
                )
            else:
                arrived.append([])
        returned = []
        for clip, parts in enumerate(shares):
            if not parts:
                returned.append([])
                continue
            starts = [
                jnp.where(me < parts, lax.rem(me - d + 2 * parts, parts), parts) * rows
                for d in range(parts)
            ]
            table = jnp.stack(starts + [plan[COUNT + clip]]).astype(jnp.int32)
            results = attention(arrived[clip], table)
            returned.append(
                [results[0]] + [rotate(parts, results[d], parts - d) for d in range(1, parts)]
            )
        totals = ()
        for clip in range(2):
            totals = assemble(clip, plan, returned[clip], qkv, totals)
        return tuple(totals)

    return run


def on_device(qkv, cotangent, lengths, target_group, target_slot):
    packed, cot = qkv[:, 0], cotangent[0]
    choices = extents(lax.axis_size("seq"), packed.shape[-1] // HEAD)
    plan, up, down = make_plan(choices, lengths, target_group, target_slot, cot)
    below, above = shift_dp(up, 1), shift_dp(down, -1)
    classes = [0] + choices
    branches = [pair_runner((a, b)) for i, a in enumerate(classes) for b in classes[: i + 1]]
    outs, grads = lax.switch(plan[BRANCH], branches, plan, packed, cot, below, above)
    up, down = pick_outputs(plan, outs)
    attended = place_outputs(plan, outs, shift_dp(up, 1), shift_dp(down, -1))
    return attended[None], grads[:, None]


def solution(mesh):
    in_specs = (P(None, "dp", None, "seq", None), P("dp", None, "seq", None), P(), P(), P())
    out_specs = (P("dp", None, "seq", None), P(None, "dp", None, "seq", None))
    return jax.shard_map(
        on_device, mesh=mesh, in_specs=in_specs, out_specs=out_specs, check_vma=False
    )
```

```python
import functools

import jax
import jax.numpy as jnp
from jax import lax
from jax.experimental import pallas as pl
from jax.experimental.pallas import tpu as pltpu
from jax.sharding import PartitionSpec as P

HEAD = 128
FACTOR = HEAD**-0.5
LOG2E = 1.4426950408889634
NEGATIVE = -1e30


SMEM = pltpu.MemorySpace.SMEM
PICK_UP, PICK_DOWN, BRANCH = 0, 1, 2
SLOT, COUNT, SOURCE, OWN = 3, 5, 7, 9
SEND_UP, SEND_DOWN, PLACE = 11, 12, 13
PLAN = 16


def shift_dp(block, distance):
    size = lax.axis_size("dp")
    route = [(i - distance, i) for i in range(size) if 0 <= i - distance < size]
    return lax.ppermute(block, "dp", route)


def extents(size, heads):
    return [p for p in range(1, size + 1) if heads % p == 0 and 2 * p >= size]


def relay(triples, sems):
    count = len(triples)
    loads = [
        pltpu.make_async_copy(source, buffer, sems.at[i])
        for i, (source, buffer, _) in enumerate(triples)
    ]
    stores = [
        pltpu.make_async_copy(buffer, target, sems.at[count + i])
        for i, (_, buffer, target) in enumerate(triples)
    ]
    for load in loads:
        load.start()
    for load, store in zip(loads, stores):
        load.wait()
        store.start()
    for store in stores:
        store.wait()


def plan_kernel(choices, rows, lengths, to_group, to_slot, cot, plan, up, down, buffers, sems):
    groups = lengths.shape[0]
    me = lax.axis_index("dp")

    def entry(group, slot):
        return lengths[group, slot] > 0, to_group[group, slot], to_slot[group, slot]

    pick_up = pick_down = send_up = send_down = jnp.int32(0)
    place = [jnp.int32(0), jnp.int32(0)]
    upper, lower = jnp.minimum(me + 1, groups - 1), jnp.maximum(me - 1, 0)
    ranks, sources, owns = [], [], []
    for slot in range(2):
        full, group, target = entry(upper, slot)
        arrives = full & (group == me) & (me + 1 < groups)
        pick_up = jnp.where(arrives, target, pick_up)
        place = [jnp.where(arrives & (target == t), 4, place[t]) for t in range(2)]
        full, group, target = entry(lower, slot)
        arrives = full & (group == me) & (me > 0)
        pick_down = jnp.where(arrives, target, pick_down)
        place = [jnp.where(arrives & (target == t), 3, place[t]) for t in range(2)]
        full, group, target = entry(me, slot)
        send_up = jnp.where(full & (group == me + 1), slot, send_up)
        send_down = jnp.where(full & (group == me - 1), slot, send_down)
        stays = full & (group == me)
        place = [jnp.where(stays & (target == t), 1 + slot, place[t]) for t in range(2)]
        sources.append(jnp.where(group == me + 1, 2, jnp.where(group == me - 1, 1, 0)))
        owns.append(target)
        count = lengths[me, slot]
        rank = jnp.where(count > 0, 1, 0)
        for p in choices[:-1]:
            rank = rank + jnp.where(count > p * rows, 1, 0)
        ranks.append(rank)
    swap = ranks[1] > ranks[0]
    first = jnp.where(swap, ranks[1], ranks[0])
    second = jnp.where(swap, ranks[0], ranks[1])
    plan[PICK_UP] = pick_up
    plan[PICK_DOWN] = pick_down
    plan[BRANCH] = first * (first + 1) // 2 + second
    for i in range(2):
        plan[SLOT + i] = jnp.where(swap, 1 - i, i)
        plan[COUNT + i] = jnp.where(swap, lengths[me, 1 - i], lengths[me, i])
        plan[SOURCE + i] = jnp.where(swap, sources[1 - i], sources[i])
        plan[OWN + i] = jnp.where(swap, owns[1 - i], owns[i])
        plan[PLACE + i] = place[i]
    plan[SEND_UP] = send_up
    plan[SEND_DOWN] = send_down
    plan[PLAN - 1] = 0
    relay(
        [(cot.at[pick_up], buffers.at[0], up), (cot.at[pick_down], buffers.at[1], down)], sems
    )


def make_plan(choices, lengths, to_group, to_slot, cot):
    block = jax.ShapeDtypeStruct(cot.shape[1:], cot.dtype)
    return pl.pallas_call(
        functools.partial(plan_kernel, choices, cot.shape[1]),
        out_shape=[jax.ShapeDtypeStruct((PLAN,), jnp.int32), block, block],
        in_specs=[pl.BlockSpec(memory_space=SMEM)] * 3 + [pl.BlockSpec(memory_space=pl.ANY)],
        out_specs=[pl.BlockSpec(memory_space=SMEM)] + [pl.BlockSpec(memory_space=pl.ANY)] * 2,
        scratch_shapes=[
            pltpu.VMEM((2,) + block.shape, block.dtype),
            pltpu.SemaphoreType.DMA((4,)),
        ],
    )(lengths, to_group, to_slot, cot)


def pick_kernel(plan, blocks, up, down, buffers, sems):
    relay(
        [
            (blocks.at[plan[SEND_UP]], buffers.at[0], up),
            (blocks.at[plan[SEND_DOWN]], buffers.at[1], down),
        ],
        sems,
    )


def pick_outputs(plan, blocks):
    block = jax.ShapeDtypeStruct(blocks.shape[1:], blocks.dtype)
    return pl.pallas_call(
        pick_kernel,
        out_shape=[block, block],
        in_specs=[pl.BlockSpec(memory_space=SMEM), pl.BlockSpec(memory_space=pl.ANY)],
        out_specs=[pl.BlockSpec(memory_space=pl.ANY)] * 2,
        scratch_shapes=[
            pltpu.VMEM((2,) + block.shape, block.dtype),
            pltpu.SemaphoreType.DMA((4,)),
        ],
    )(plan, blocks)


def place_kernel(plan, blocks, below, above, out, buffers, sems):
    for t in range(2):
        buffer = buffers.at[t]
        code = plan[PLACE + t]

        @pl.when(code == 0)
        def _():
            buffer[...] = jnp.zeros_like(buffer)

        for number, source in enumerate([blocks.at[0], blocks.at[1], below, above], 1):

            @pl.when(code == number)
            def _():
                pltpu.make_async_copy(source, buffer, sems.at[t]).start()

    stores = []
    for t in range(2):
        buffer = buffers.at[t]

        @pl.when(plan[PLACE + t] > 0)
        def _():
            pltpu.make_async_copy(below, buffer, sems.at[t]).wait()

        stores.append(pltpu.make_async_copy(buffer, out.at[t], sems.at[2 + t]))
        stores[-1].start()
    for store in stores:
        store.wait()


def place_outputs(plan, blocks, below, above):
    return pl.pallas_call(
        place_kernel,
        out_shape=jax.ShapeDtypeStruct(blocks.shape, blocks.dtype),
        in_specs=[pl.BlockSpec(memory_space=SMEM)] + [pl.BlockSpec(memory_space=pl.ANY)] * 3,
        out_specs=pl.BlockSpec(memory_space=pl.ANY),
        scratch_shapes=[
            pltpu.VMEM(blocks.shape, blocks.dtype),
            pltpu.SemaphoreType.DMA((4,)),
        ],
    )(plan, blocks, below, above)


def pack_kernel(parts, clip, plan, qkv, cot, below, above, *refs):
    pieces, buffers, sems = refs[:parts], refs[parts], refs[parts + 1]
    width = pieces[0].shape[2]
    me = lax.axis_index("seq")
    slot, source, own = plan[SLOT + clip], plan[SOURCE + clip], plan[OWN + clip]

    def columns(d):
        return pl.ds(pl.multiple_of(lax.rem(me + d, parts) * width, HEAD), width)

    loads = [
        pltpu.make_async_copy(
            qkv.at[:, slot, :, columns(d)], buffers.at[d, pl.ds(0, 3)], sems.at[d]
        )
        for d in range(parts)
    ]
    for load in loads:
        load.start()
    for code, block in enumerate([cot.at[own], below, above]):

        @pl.when(source == code)
        def _():
            for d in range(parts):
                pltpu.make_async_copy(
                    block.at[:, columns(d)], buffers.at[d, 3], sems.at[parts + d]
                ).start()

    stores = []
    for d in list(range(1, parts)) + [0]:
        loads[d].wait()
        pltpu.make_async_copy(
            below.at[:, columns(d)], buffers.at[d, 3], sems.at[parts + d]
        ).wait()
        stores.append(pltpu.make_async_copy(buffers.at[d], pieces[d], sems.at[2 * parts + d]))
        stores[-1].start()
    for store in stores:
        store.wait()


def pack(parts, clip, plan, qkv, cot, below, above):
    rows, features = below.shape
    piece = jax.ShapeDtypeStruct((4, rows, features // parts), qkv.dtype)
    return pl.pallas_call(
        functools.partial(pack_kernel, parts, clip),
        out_shape=[piece] * parts,
        in_specs=[pl.BlockSpec(memory_space=SMEM)] + [pl.BlockSpec(memory_space=pl.ANY)] * 4,
        out_specs=[pl.BlockSpec(memory_space=pl.ANY)] * parts,
        scratch_shapes=[
            pltpu.VMEM((parts,) + piece.shape, piece.dtype),
            pltpu.SemaphoreType.DMA((3 * parts,)),
        ],
    )(plan, qkv, cot, below, above)


def assemble_kernel(parts, clip, plan, *refs):
    outs, grads, buffers, sems = refs[-4:]
    slot = plan[SLOT + clip]
    me = lax.axis_index("seq")
    if not parts:
        buffers[...] = jnp.zeros_like(buffers)
        targets = [outs.at[slot]] + [grads.at[i, slot] for i in range(3)]
        stores = [
            pltpu.make_async_copy(buffers, target, sems.at[i]) for i, target in enumerate(targets)
        ]
        for store in stores:
            store.start()
        for store in stores:
            store.wait()
        return
    width = refs[0].shape[2]
    triples = []
    for d in range(parts):
        columns = pl.ds(pl.multiple_of(lax.rem(me + d, parts) * width, HEAD), width)
        triples.append((refs[d].at[0], buffers.at[d, 0], outs.at[slot, :, columns]))
        rest = pl.ds(1, 3)
        triples.append((refs[d].at[rest], buffers.at[d, rest], grads.at[:, slot, :, columns]))
    relay(triples, sems)


def assemble(clip, plan, pieces, qkv, totals):
    parts = len(pieces)
    rows, features = qkv.shape[2:]
    any_space = pl.BlockSpec(memory_space=pl.ANY)
    operands = list(pieces) + list(totals)
    aliases = {1 + parts + i: i for i in range(len(totals))}
    return pl.pallas_call(
        functools.partial(assemble_kernel, parts, clip),
        out_shape=[
            jax.ShapeDtypeStruct(qkv.shape[1:], qkv.dtype),
            jax.ShapeDtypeStruct(qkv.shape, qkv.dtype),
        ],
        in_specs=[pl.BlockSpec(memory_space=SMEM)] + [any_space] * len(operands),
        out_specs=[any_space] * 2,
        scratch_shapes=[
            pltpu.VMEM(
                (parts,) + pieces[0].shape if parts else (rows, features), qkv.dtype
            ),
            pltpu.SemaphoreType.DMA((max(4 * parts, 4),)),
        ],
        input_output_aliases=aliases,
    )(plan, *operands)


def attention_kernel(parts, plan_ref, *refs):
    ins, outs = refs[:parts], refs[parts:]
    rows = ins[0].shape[1]
    extent = parts * rows
    count = plan_ref[parts]
    row_iota = lax.broadcasted_iota(jnp.int32, (rows, 1), 0)
    inside = jnp.concatenate([row_iota + plan_ref[d] < count for d in range(parts)], axis=0)

    def load(which):
        return jnp.concatenate([r[which] for r in ins], axis=0)

    q, k, v, g = load(0), load(1), load(2), load(3)
    g = jnp.where(inside, g, jnp.zeros((), g.dtype))
    nt = (((1,), (1,)), ((), ()))
    tn = (((0,), (0,)), ((), ()))
    nn = (((1,), (0,)), ((), ()))
    dot = functools.partial(lax.dot_general, preferred_element_type=jnp.float32)
    grad_k = grad_v = None
    out_rows, grad_q_rows = [], []
    step = min(256, extent)
    for start in range(0, extent, step):
        stop = min(start + step, extent)
        q_i, g_i = q[start:stop], g[start:stop]
        scores = jnp.where(inside, dot(k, q_i, nt), NEGATIVE)
        largest = jnp.max(scores, axis=0, keepdims=True)
        exponent = jnp.exp2((scores - largest) * (FACTOR * LOG2E))
        weights = exponent * (1.0 / jnp.sum(exponent, axis=0, keepdims=True))
        rounded = weights.astype(jnp.bfloat16)
        grad_weights = dot(v, g_i, nt)
        inner = jnp.sum(grad_weights * weights, axis=0, keepdims=True)
        score_grad = (weights * (grad_weights - inner)).astype(jnp.bfloat16)
        out_rows.append(dot(v, rounded, tn).T)
        grad_q_rows.append(dot(k, score_grad, tn).T)
        add_k = dot(score_grad, q_i, nn)
        add_v = dot(rounded, g_i, nn)
        grad_k = add_k if grad_k is None else grad_k + add_k
        grad_v = add_v if grad_v is None else grad_v + add_v
    out = jnp.where(inside, jnp.concatenate(out_rows, axis=0), 0.0).astype(jnp.bfloat16)
    grad_q = (jnp.concatenate(grad_q_rows, axis=0) * FACTOR).astype(jnp.bfloat16)
    grad_k = (grad_k * FACTOR).astype(jnp.bfloat16)
    grad_v = grad_v.astype(jnp.bfloat16)
    for d, ref in enumerate(outs):
        span = slice(d * rows, (d + 1) * rows)
        ref[0] = out[span]
        ref[1] = grad_q[span]
        ref[2] = grad_k[span]
        ref[3] = grad_v[span]


def attention(pieces, plan):
    parts = len(pieces)
    fields, rows, width = pieces[0].shape
    spec = pl.BlockSpec((fields, rows, HEAD), lambda h, plan: (0, 0, h))
    return pl.pallas_call(
        functools.partial(attention_kernel, parts),
        out_shape=[jax.ShapeDtypeStruct(p.shape, p.dtype) for p in pieces],
        grid_spec=pltpu.PrefetchScalarGridSpec(
            num_scalar_prefetch=1,
            grid=(width // HEAD,),
            in_specs=[spec] * parts,
            out_specs=[spec] * parts,
        ),
        compiler_params=pltpu.CompilerParams(vmem_limit_bytes=40 * 2**20),
        cost_estimate=pl.CostEstimate(
            flops=12 * (parts * rows) ** 2 * width,
            bytes_accessed=16 * parts * rows * width,
            transcendentals=(parts * rows) ** 2 * (width // HEAD),
        ),
    )(plan, *pieces)


def rotate(parts, block, distance):
    return lax.ppermute(block, "seq", [(i, (i + distance) % parts) for i in range(parts)])


def pair_runner(shares):
    def run(plan, qkv, cot, below, above):
        rows = below.shape[0]
        me = lax.axis_index("seq")
        arrived = []
        for clip, parts in enumerate(shares):
            if parts:
                pieces = pack(parts, clip, plan, qkv, cot, below, above)
                arrived.append(
                    [pieces[0]] + [rotate(parts, pieces[d], d) for d in range(1, parts)]
                )
            else:
                arrived.append([])
        returned = []
        for clip, parts in enumerate(shares):
            if not parts:
                returned.append([])
                continue
            starts = [
                jnp.where(me < parts, lax.rem(me - d + 2 * parts, parts), parts) * rows
                for d in range(parts)
            ]
            table = jnp.stack(starts + [plan[COUNT + clip]]).astype(jnp.int32)
            results = attention(arrived[clip], table)
            returned.append(
                [results[0]] + [rotate(parts, results[d], parts - d) for d in range(1, parts)]
            )
        totals = ()
        for clip in range(2):
            totals = assemble(clip, plan, returned[clip], qkv, totals)
        return tuple(totals)

    return run


def on_device(qkv, cotangent, lengths, target_group, target_slot):
    packed, cot = qkv[:, 0], cotangent[0]
    choices = extents(lax.axis_size("seq"), packed.shape[-1] // HEAD)
    plan, up, down = make_plan(choices, lengths, target_group, target_slot, cot)
    below, above = shift_dp(up, 1), shift_dp(down, -1)
    classes = [0] + choices
    branches = [pair_runner((a, b)) for i, a in enumerate(classes) for b in classes[: i + 1]]
    outs, grads = lax.switch(plan[BRANCH], branches, plan, packed, cot, below, above)
    up, down = pick_outputs(plan, outs)
    attended = place_outputs(plan, outs, shift_dp(up, 1), shift_dp(down, -1))
    return attended[None], grads[:, None]


def solution(mesh):
    in_specs = (P(None, "dp", None, "seq", None), P("dp", None, "seq", None), P(), P(), P())
    out_specs = (P("dp", None, "seq", None), P(None, "dp", None, "seq", None))
    return jax.shard_map(
        on_device, mesh=mesh, in_specs=in_specs, out_specs=out_specs, check_vma=False
    )
```

```python
import functools

import jax
import jax.numpy as jnp
from jax import lax
from jax.experimental import pallas as pl
from jax.experimental.pallas import tpu as pltpu
from jax.sharding import PartitionSpec as P

HEAD = 128
FACTOR = HEAD**-0.5
LOG2E = 1.4426950408889634
NEGATIVE = -1e30


SMEM = pltpu.MemorySpace.SMEM
PICK_UP, PICK_DOWN, BRANCH = 0, 1, 2
SLOT, COUNT, SOURCE, OWN = 3, 5, 7, 9
SEND_UP, SEND_DOWN, PLACE = 11, 12, 13
PLAN = 16


def shift_dp(block, distance):
    size = lax.axis_size("dp")
    route = [(i - distance, i) for i in range(size) if 0 <= i - distance < size]
    return lax.ppermute(block, "dp", route)


def extents(size, heads, rows):
    classes = []
    for p in range(1, size + 1):
        if heads % p or 2 * p < size:
            continue
        for extra in (0, rows // 2, rows) if size <= 4 else (0, rows):
            limit = p * rows + extra
            if (limit < size * rows or p == size and not extra) and (
                not classes or limit > capacity(classes[-1], rows)
            ):
                classes.append((p, extra))
    return classes


def capacity(share, rows):
    return share[0] * rows + share[1]


def relay(triples, sems):
    count = len(triples)
    loads = [
        pltpu.make_async_copy(source, buffer, sems.at[i])
        for i, (source, buffer, _) in enumerate(triples)
    ]
    stores = [
        pltpu.make_async_copy(buffer, target, sems.at[count + i])
        for i, (_, buffer, target) in enumerate(triples)
    ]
    for load in loads:
        load.start()
    for load, store in zip(loads, stores):
        load.wait()
        store.start()
    for store in stores:
        store.wait()


def plan_kernel(choices, rows, lengths, to_group, to_slot, cot, plan, up, down, buffers, sems):
    groups = lengths.shape[0]
    me = lax.axis_index("dp")

    def entry(group, slot):
        return lengths[group, slot] > 0, to_group[group, slot], to_slot[group, slot]

    pick_up = pick_down = send_up = send_down = jnp.int32(0)
    place = [jnp.int32(0), jnp.int32(0)]
    upper, lower = jnp.minimum(me + 1, groups - 1), jnp.maximum(me - 1, 0)
    ranks, sources, owns = [], [], []
    for slot in range(2):
        full, group, target = entry(upper, slot)
        arrives = full & (group == me) & (me + 1 < groups)
        pick_up = jnp.where(arrives, target, pick_up)
        place = [jnp.where(arrives & (target == t), 4, place[t]) for t in range(2)]
        full, group, target = entry(lower, slot)
        arrives = full & (group == me) & (me > 0)
        pick_down = jnp.where(arrives, target, pick_down)
        place = [jnp.where(arrives & (target == t), 3, place[t]) for t in range(2)]
        full, group, target = entry(me, slot)
        send_up = jnp.where(full & (group == me + 1), slot, send_up)
        send_down = jnp.where(full & (group == me - 1), slot, send_down)
        stays = full & (group == me)
        place = [jnp.where(stays & (target == t), 1 + slot, place[t]) for t in range(2)]
        sources.append(jnp.where(group == me + 1, 2, jnp.where(group == me - 1, 1, 0)))
        owns.append(target)
        count = lengths[me, slot]
        rank = jnp.where(count > 0, 1, 0)
        for p in choices[:-1]:
            rank = rank + jnp.where(count > capacity(p, rows), 1, 0)
        ranks.append(rank)
    swap = ranks[1] > ranks[0]
    first = jnp.where(swap, ranks[1], ranks[0])
    second = jnp.where(swap, ranks[0], ranks[1])
    plan[PICK_UP] = pick_up
    plan[PICK_DOWN] = pick_down
    plan[BRANCH] = first * (first + 1) // 2 + second
    for i in range(2):
        plan[SLOT + i] = jnp.where(swap, 1 - i, i)
        plan[COUNT + i] = jnp.where(swap, lengths[me, 1 - i], lengths[me, i])
        plan[SOURCE + i] = jnp.where(swap, sources[1 - i], sources[i])
        plan[OWN + i] = jnp.where(swap, owns[1 - i], owns[i])
        plan[PLACE + i] = place[i]
    plan[SEND_UP] = send_up
    plan[SEND_DOWN] = send_down
    plan[PLAN - 1] = 0
    relay(
        [(cot.at[pick_up], buffers.at[0], up), (cot.at[pick_down], buffers.at[1], down)], sems
    )


def make_plan(choices, lengths, to_group, to_slot, cot):
    block = jax.ShapeDtypeStruct(cot.shape[1:], cot.dtype)
    return pl.pallas_call(
        functools.partial(plan_kernel, choices, cot.shape[1]),
        out_shape=[jax.ShapeDtypeStruct((PLAN,), jnp.int32), block, block],
        in_specs=[pl.BlockSpec(memory_space=SMEM)] * 3 + [pl.BlockSpec(memory_space=pl.ANY)],
        out_specs=[pl.BlockSpec(memory_space=SMEM)] + [pl.BlockSpec(memory_space=pl.ANY)] * 2,
        scratch_shapes=[
            pltpu.VMEM((2,) + block.shape, block.dtype),
            pltpu.SemaphoreType.DMA((4,)),
        ],
    )(lengths, to_group, to_slot, cot)


def pick_kernel(plan, blocks, up, down, buffers, sems):
    relay(
        [
            (blocks.at[plan[SEND_UP]], buffers.at[0], up),
            (blocks.at[plan[SEND_DOWN]], buffers.at[1], down),
        ],
        sems,
    )


def pick_outputs(plan, blocks):
    block = jax.ShapeDtypeStruct(blocks.shape[1:], blocks.dtype)
    return pl.pallas_call(
        pick_kernel,
        out_shape=[block, block],
        in_specs=[pl.BlockSpec(memory_space=SMEM), pl.BlockSpec(memory_space=pl.ANY)],
        out_specs=[pl.BlockSpec(memory_space=pl.ANY)] * 2,
        scratch_shapes=[
            pltpu.VMEM((2,) + block.shape, block.dtype),
            pltpu.SemaphoreType.DMA((4,)),
        ],
    )(plan, blocks)


def place_kernel(plan, blocks, below, above, out, buffers, sems):
    for t in range(2):
        buffer = buffers.at[t]
        code = plan[PLACE + t]

        @pl.when(code == 0)
        def _():
            buffer[...] = jnp.zeros_like(buffer)

        for number, source in enumerate([blocks.at[0], blocks.at[1], below, above], 1):

            @pl.when(code == number)
            def _():
                pltpu.make_async_copy(source, buffer, sems.at[t]).start()

    stores = []
    for t in range(2):
        buffer = buffers.at[t]

        @pl.when(plan[PLACE + t] > 0)
        def _():
            pltpu.make_async_copy(below, buffer, sems.at[t]).wait()

        stores.append(pltpu.make_async_copy(buffer, out.at[t], sems.at[2 + t]))
        stores[-1].start()
    for store in stores:
        store.wait()


def place_outputs(plan, blocks, below, above):
    return pl.pallas_call(
        place_kernel,
        out_shape=jax.ShapeDtypeStruct(blocks.shape, blocks.dtype),
        in_specs=[pl.BlockSpec(memory_space=SMEM)] + [pl.BlockSpec(memory_space=pl.ANY)] * 3,
        out_specs=pl.BlockSpec(memory_space=pl.ANY),
        scratch_shapes=[
            pltpu.VMEM(blocks.shape, blocks.dtype),
            pltpu.SemaphoreType.DMA((4,)),
        ],
    )(plan, blocks, below, above)


def pack_kernel(parts, clip, plan, qkv, cot, below, above, *refs):
    pieces, buffers, sems = refs[:parts], refs[parts], refs[parts + 1]
    width = pieces[0].shape[2]
    me = lax.axis_index("seq")
    slot, source, own = plan[SLOT + clip], plan[SOURCE + clip], plan[OWN + clip]

    def columns(d):
        return pl.ds(pl.multiple_of(lax.rem(me + d, parts) * width, HEAD), width)

    loads = [
        pltpu.make_async_copy(
            qkv.at[:, slot, :, columns(d)], buffers.at[d, pl.ds(0, 3)], sems.at[d]
        )
        for d in range(parts)
    ]
    for load in loads:
        load.start()
    for code, block in enumerate([cot.at[own], below, above]):

        @pl.when(source == code)
        def _():
            for d in range(parts):
                pltpu.make_async_copy(
                    block.at[:, columns(d)], buffers.at[d, 3], sems.at[parts + d]
                ).start()

    stores = []
    for d in list(range(1, parts)) + [0]:
        loads[d].wait()
        pltpu.make_async_copy(
            below.at[:, columns(d)], buffers.at[d, 3], sems.at[parts + d]
        ).wait()
        stores.append(pltpu.make_async_copy(buffers.at[d], pieces[d], sems.at[2 * parts + d]))
        stores[-1].start()
    for store in stores:
        store.wait()


def pack(parts, clip, plan, qkv, cot, below, above):
    rows, features = below.shape
    piece = jax.ShapeDtypeStruct((4, rows, features // parts), qkv.dtype)
    return pl.pallas_call(
        functools.partial(pack_kernel, parts, clip),
        out_shape=[piece] * parts,
        in_specs=[pl.BlockSpec(memory_space=SMEM)] + [pl.BlockSpec(memory_space=pl.ANY)] * 4,
        out_specs=[pl.BlockSpec(memory_space=pl.ANY)] * parts,
        scratch_shapes=[
            pltpu.VMEM((parts,) + piece.shape, piece.dtype),
            pltpu.SemaphoreType.DMA((3 * parts,)),
        ],
    )(plan, qkv, cot, below, above)


def assemble_kernel(share, clip, plan, *refs):
    parts, extra = share
    outs, grads, buffers, sems = refs[-4:]
    slot = plan[SLOT + clip]
    me = lax.axis_index("seq")

    def column(c):
        width = refs[0].shape[2]
        return pl.ds(pl.multiple_of(c * width, HEAD), width)

    def chunks():
        triples = []
        for d in range(parts):
            columns = column(lax.rem(me + d, parts))
            rest = pl.ds(1, 3)
            triples.append((refs[d].at[0], buffers.at[d, 0], outs.at[slot, :, columns]))
            triples.append((refs[d].at[rest], buffers.at[d, rest], grads.at[:, slot, :, columns]))
        relay(triples, sems)

    def further_block():
        span = pl.ds(0, extra)
        rows = buffers.shape[2]
        if extra < rows:
            buffers[:, :, extra:, :] = jnp.zeros(
                (parts, 4, rows - extra, buffers.shape[3]), buffers.dtype
            )
        loads, stores = [], []
        for c in range(parts):
            loads.append(
                pltpu.make_async_copy(refs[parts + c], buffers.at[c, :, span], sems.at[c])
            )
            loads[-1].start()
        for c in range(parts):
            loads[c].wait()
            columns = column(c)
            stores.append(
                pltpu.make_async_copy(
                    buffers.at[c, 0], outs.at[slot, :, columns], sems.at[parts + c]
                )
            )
            stores.append(
                pltpu.make_async_copy(
                    buffers.at[c, pl.ds(1, 3)],
                    grads.at[:, slot, :, columns],
                    sems.at[2 * parts + c],
                )
            )
            stores[-2].start()
            stores[-1].start()
        for store in stores:
            store.wait()

    if not parts:
        buffers[...] = jnp.zeros_like(buffers)
        targets = [outs.at[slot]] + [grads.at[i, slot] for i in range(3)]
        stores = [
            pltpu.make_async_copy(buffers, target, sems.at[i]) for i, target in enumerate(targets)
        ]
        for store in stores:
            store.start()
        for store in stores:
            store.wait()
    elif not extra:
        chunks()
    else:
        pl.when(me < parts)(chunks)
        pl.when(me >= parts)(further_block)


def assemble(share, clip, plan, pieces, qkv, totals):
    parts = share[0]
    rows, features = qkv.shape[2:]
    any_space = pl.BlockSpec(memory_space=pl.ANY)
    operands = list(pieces) + list(totals)
    aliases = {1 + len(pieces) + i: i for i in range(len(totals))}
    return pl.pallas_call(
        functools.partial(assemble_kernel, share, clip),
        out_shape=[
            jax.ShapeDtypeStruct(qkv.shape[1:], qkv.dtype),
            jax.ShapeDtypeStruct(qkv.shape, qkv.dtype),
        ],
        in_specs=[pl.BlockSpec(memory_space=SMEM)] + [any_space] * len(operands),
        out_specs=[any_space] * 2,
        scratch_shapes=[
            pltpu.VMEM(
                (parts,) + pieces[0].shape if parts else (rows, features), qkv.dtype
            ),
            pltpu.SemaphoreType.DMA((max(4 * parts, 4),)),
        ],
        input_output_aliases=aliases,
    )(plan, *operands)


def attention_kernel(parts, plan_ref, *refs):
    ins, outs = refs[:parts], refs[parts:]
    sizes = [r.shape[1] for r in ins]
    extent = sum(sizes)
    count = plan_ref[parts]
    inside = jnp.concatenate(
        [
            lax.broadcasted_iota(jnp.int32, (size, 1), 0) + plan_ref[d] < count
            for d, size in enumerate(sizes)
        ],
        axis=0,
    )

    def load(which):
        return jnp.concatenate([r[which] for r in ins], axis=0)

    q, k, v, g = load(0), load(1), load(2), load(3)
    g = jnp.where(inside, g, jnp.zeros((), g.dtype))
    nt = (((1,), (1,)), ((), ()))
    tn = (((0,), (0,)), ((), ()))
    nn = (((1,), (0,)), ((), ()))
    dot = functools.partial(lax.dot_general, preferred_element_type=jnp.float32)
    grad_k = grad_v = None
    out_rows, grad_q_rows = [], []
    step = extent if extent < 384 else 256
    for start in range(0, extent, step):
        stop = min(start + step, extent)
        q_i, g_i = q[start:stop], g[start:stop]
        scores = jnp.where(inside, dot(k, q_i, nt), NEGATIVE)
        largest = jnp.max(scores, axis=0, keepdims=True)
        exponent = jnp.exp2((scores - largest) * (FACTOR * LOG2E))
        weights = exponent * (1.0 / jnp.sum(exponent, axis=0, keepdims=True))
        rounded = weights.astype(jnp.bfloat16)
        grad_weights = dot(v, g_i, nt)
        inner = jnp.sum(grad_weights * weights, axis=0, keepdims=True)
        score_grad = (weights * (grad_weights - inner)).astype(jnp.bfloat16)
        out_rows.append(dot(v, rounded, tn).T)
        grad_q_rows.append(dot(k, score_grad, tn).T)
        add_k = dot(score_grad, q_i, nn)
        add_v = dot(rounded, g_i, nn)
        grad_k = add_k if grad_k is None else grad_k + add_k
        grad_v = add_v if grad_v is None else grad_v + add_v
    out = jnp.where(inside, jnp.concatenate(out_rows, axis=0), 0.0).astype(jnp.bfloat16)
    grad_q = (jnp.concatenate(grad_q_rows, axis=0) * FACTOR).astype(jnp.bfloat16)
    grad_k = (grad_k * FACTOR).astype(jnp.bfloat16)
    grad_v = grad_v.astype(jnp.bfloat16)
    for d, ref in enumerate(outs):
        span = slice(sum(sizes[:d]), sum(sizes[: d + 1]))
        ref[0] = out[span]
        ref[1] = grad_q[span]
        ref[2] = grad_k[span]
        ref[3] = grad_v[span]


def attention(pieces, plan):
    parts = len(pieces)
    width = pieces[0].shape[2]
    extent = sum(p.shape[1] for p in pieces)
    specs = [pl.BlockSpec((4, p.shape[1], HEAD), lambda h, plan: (0, 0, h)) for p in pieces]
    return pl.pallas_call(
        functools.partial(attention_kernel, parts),
        out_shape=[jax.ShapeDtypeStruct(p.shape, p.dtype) for p in pieces],
        grid_spec=pltpu.PrefetchScalarGridSpec(
            num_scalar_prefetch=1,
            grid=(width // HEAD,),
            in_specs=specs,
            out_specs=specs,
        ),
        compiler_params=pltpu.CompilerParams(vmem_limit_bytes=40 * 2**20),
        cost_estimate=pl.CostEstimate(
            flops=12 * extent**2 * width,
            bytes_accessed=16 * extent * width,
            transcendentals=extent**2 * (width // HEAD),
        ),
    )(plan, *pieces)


def rotate(parts, block, distance):
    return lax.ppermute(block, "seq", [(i, (i + distance) % parts) for i in range(parts)])


def pair_runner(shares):
    def run(plan, qkv, cot, below, above):
        rows = below.shape[0]
        end = rows * lax.axis_size("seq")
        me = lax.axis_index("seq")
        arrived = []
        for clip, (parts, extra) in enumerate(shares):
            if not parts:
                arrived.append([])
                continue
            pieces = pack(parts, clip, plan, qkv, cot, below, above)
            here = [pieces[0]] + [rotate(parts, pieces[d], d) for d in range(1, parts)]
            if extra:
                further = [
                    lax.ppermute(pieces[c][:, :extra], "seq", [(parts, c)]) for c in range(parts)
                ]
                block = further[0]
                for c in range(1, parts):
                    block = jnp.where(me == c, further[c], block)
                here.append(block)
            arrived.append(here)
        returned = []
        for clip, (parts, extra) in enumerate(shares):
            if not parts:
                returned.append([])
                continue
            starts = [lax.rem(me - d + 2 * parts, parts) * rows for d in range(parts)]
            if extra:
                starts.append(jnp.int32(parts * rows))
            starts = [jnp.where(me < parts, start, end) for start in starts]
            table = jnp.stack(starts + [plan[COUNT + clip]]).astype(jnp.int32)
            results = attention(arrived[clip], table)
            back = [results[0]] + [rotate(parts, results[d], parts - d) for d in range(1, parts)]
            if extra:
                back += [lax.ppermute(results[parts], "seq", [(c, parts)]) for c in range(parts)]
            returned.append(back)
        totals = ()
        for clip in range(2):
            totals = assemble(shares[clip], clip, plan, returned[clip], qkv, totals)
        return tuple(totals)

    return run


def on_device(qkv, cotangent, lengths, target_group, target_slot):
    packed, cot = qkv[:, 0], cotangent[0]
    choices = extents(lax.axis_size("seq"), packed.shape[-1] // HEAD, packed.shape[2])
    plan, up, down = make_plan(choices, lengths, target_group, target_slot, cot)
    below, above = shift_dp(up, 1), shift_dp(down, -1)
    classes = [(0, 0)] + choices
    branches = [pair_runner((a, b)) for i, a in enumerate(classes) for b in classes[: i + 1]]
    outs, grads = lax.switch(plan[BRANCH], branches, plan, packed, cot, below, above)
    up, down = pick_outputs(plan, outs)
    attended = place_outputs(plan, outs, shift_dp(up, 1), shift_dp(down, -1))
    return attended[None], grads[:, None]


def solution(mesh):
    in_specs = (P(None, "dp", None, "seq", None), P("dp", None, "seq", None), P(), P(), P())
    out_specs = (P("dp", None, "seq", None), P(None, "dp", None, "seq", None))
    return jax.shard_map(
        on_device, mesh=mesh, in_specs=in_specs, out_specs=out_specs, check_vma=False
    )
```

```python
import functools

import jax
import jax.numpy as jnp
from jax import lax
from jax.experimental import pallas as pl
from jax.experimental.pallas import tpu as pltpu
from jax.sharding import PartitionSpec as P

HEAD = 128
FACTOR = HEAD**-0.5
LOG2E = 1.4426950408889634
NEGATIVE = -1e30


SMEM = pltpu.MemorySpace.SMEM
PICK_UP, PICK_DOWN, BRANCH = 0, 1, 2
SLOT, COUNT, SOURCE, OWN = 3, 5, 7, 9
SEND_UP, SEND_DOWN, PLACE = 11, 12, 13
PLAN = 16


def shift_dp(block, distance):
    size = lax.axis_size("dp")
    route = [(i - distance, i) for i in range(size) if 0 <= i - distance < size]
    return lax.ppermute(block, "dp", route)


def extents(size, heads):
    return [p for p in range(1, size + 1) if heads % p == 0 and 2 * p >= size]


def relay(triples, sems):
    count = len(triples)
    loads = [
        pltpu.make_async_copy(source, buffer, sems.at[i])
        for i, (source, buffer, _) in enumerate(triples)
    ]
    stores = [
        pltpu.make_async_copy(buffer, target, sems.at[count + i])
        for i, (_, buffer, target) in enumerate(triples)
    ]
    for load in loads:
        load.start()
    for load, store in zip(loads, stores):
        load.wait()
        store.start()
    for store in stores:
        store.wait()


def plan_kernel(choices, rows, tables, cot, plan, up, down, buffers, sems):
    groups = tables.shape[1]
    me = lax.axis_index("dp")

    def entry(group, slot):
        return tables[0, group, slot] > 0, tables[1, group, slot], tables[2, group, slot]

    pick_up = pick_down = send_up = send_down = jnp.int32(0)
    place = [jnp.int32(0), jnp.int32(0)]
    upper, lower = jnp.minimum(me + 1, groups - 1), jnp.maximum(me - 1, 0)
    ranks, sources, owns = [], [], []
    for slot in range(2):
        full, group, target = entry(upper, slot)
        arrives = full & (group == me) & (me + 1 < groups)
        pick_up = jnp.where(arrives, target, pick_up)
        place = [jnp.where(arrives & (target == t), 4, place[t]) for t in range(2)]
        full, group, target = entry(lower, slot)
        arrives = full & (group == me) & (me > 0)
        pick_down = jnp.where(arrives, target, pick_down)
        place = [jnp.where(arrives & (target == t), 3, place[t]) for t in range(2)]
        full, group, target = entry(me, slot)
        send_up = jnp.where(full & (group == me + 1), slot, send_up)
        send_down = jnp.where(full & (group == me - 1), slot, send_down)
        stays = full & (group == me)
        place = [jnp.where(stays & (target == t), 1 + slot, place[t]) for t in range(2)]
        sources.append(jnp.where(group == me + 1, 2, jnp.where(group == me - 1, 1, 0)))
        owns.append(target)
        count = tables[0, me, slot]
        rank = jnp.where(count > 0, 1, 0)
        for p in choices[:-1]:
            rank = rank + jnp.where(count > p * rows, 1, 0)
        ranks.append(rank)
    swap = ranks[1] > ranks[0]
    first = jnp.where(swap, ranks[1], ranks[0])
    second = jnp.where(swap, ranks[0], ranks[1])
    plan[PICK_UP] = pick_up
    plan[PICK_DOWN] = pick_down
    plan[BRANCH] = first * (first + 1) // 2 + second
    for i in range(2):
        plan[SLOT + i] = jnp.where(swap, 1 - i, i)
        plan[COUNT + i] = jnp.where(swap, tables[0, me, 1 - i], tables[0, me, i])
        plan[SOURCE + i] = jnp.where(swap, sources[1 - i], sources[i])
        plan[OWN + i] = jnp.where(swap, owns[1 - i], owns[i])
        plan[PLACE + i] = place[i]
    plan[SEND_UP] = send_up
    plan[SEND_DOWN] = send_down
    plan[PLAN - 1] = 0
    relay(
        [(cot.at[pick_up], buffers.at[0], up), (cot.at[pick_down], buffers.at[1], down)], sems
    )


def make_plan(choices, tables, cot):
    block = jax.ShapeDtypeStruct(cot.shape[1:], cot.dtype)
    return pl.pallas_call(
        functools.partial(plan_kernel, choices, cot.shape[1]),
        out_shape=[jax.ShapeDtypeStruct((PLAN,), jnp.int32), block, block],
        in_specs=[pl.BlockSpec(memory_space=SMEM), pl.BlockSpec(memory_space=pl.ANY)],
        out_specs=[pl.BlockSpec(memory_space=SMEM)] + [pl.BlockSpec(memory_space=pl.ANY)] * 2,
        scratch_shapes=[
            pltpu.VMEM((2,) + block.shape, block.dtype),
            pltpu.SemaphoreType.DMA((4,)),
        ],
    )(tables, cot)


def pick_kernel(plan, blocks, up, down, buffers, sems):
    relay(
        [
            (blocks.at[plan[SEND_UP]], buffers.at[0], up),
            (blocks.at[plan[SEND_DOWN]], buffers.at[1], down),
        ],
        sems,
    )


def pick_outputs(plan, blocks):
    block = jax.ShapeDtypeStruct(blocks.shape[1:], blocks.dtype)
    return pl.pallas_call(
        pick_kernel,
        out_shape=[block, block],
        in_specs=[pl.BlockSpec(memory_space=SMEM), pl.BlockSpec(memory_space=pl.ANY)],
        out_specs=[pl.BlockSpec(memory_space=pl.ANY)] * 2,
        scratch_shapes=[
            pltpu.VMEM((2,) + block.shape, block.dtype),
            pltpu.SemaphoreType.DMA((4,)),
        ],
    )(plan, blocks)


def place_kernel(plan, blocks, below, above, out, buffers, sems):
    for t in range(2):
        buffer = buffers.at[t]
        code = plan[PLACE + t]

        @pl.when(code == 0)
        def _():
            buffer[...] = jnp.zeros_like(buffer)

        for number, source in enumerate([blocks.at[0], blocks.at[1], below, above], 1):

            @pl.when(code == number)
            def _():
                pltpu.make_async_copy(source, buffer, sems.at[t]).start()

    stores = []
    for t in range(2):
        buffer = buffers.at[t]

        @pl.when(plan[PLACE + t] > 0)
        def _():
            pltpu.make_async_copy(below, buffer, sems.at[t]).wait()

        stores.append(pltpu.make_async_copy(buffer, out.at[t], sems.at[2 + t]))
        stores[-1].start()
    for store in stores:
        store.wait()


def place_outputs(plan, blocks, below, above):
    return pl.pallas_call(
        place_kernel,
        out_shape=jax.ShapeDtypeStruct(blocks.shape, blocks.dtype),
        in_specs=[pl.BlockSpec(memory_space=SMEM)] + [pl.BlockSpec(memory_space=pl.ANY)] * 3,
        out_specs=pl.BlockSpec(memory_space=pl.ANY),
        scratch_shapes=[
            pltpu.VMEM(blocks.shape, blocks.dtype),
            pltpu.SemaphoreType.DMA((4,)),
        ],
    )(plan, blocks, below, above)


def pack_kernel(parts, clip, plan, qkv, cot, below, above, *refs):
    pieces, buffers, sems = refs[:parts], refs[parts], refs[parts + 1]
    width = pieces[0].shape[2]
    me = lax.axis_index("seq")
    slot, source, own = plan[SLOT + clip], plan[SOURCE + clip], plan[OWN + clip]

    def columns(d):
        return pl.ds(pl.multiple_of(lax.rem(me + d, parts) * width, HEAD), width)

    loads = [
        pltpu.make_async_copy(
            qkv.at[:, slot, :, columns(d)], buffers.at[d, pl.ds(0, 3)], sems.at[d]
        )
        for d in range(parts)
    ]
    for load in loads:
        load.start()
    for code, block in enumerate([cot.at[own], below, above]):

        @pl.when(source == code)
        def _():
            for d in range(parts):
                pltpu.make_async_copy(
                    block.at[:, columns(d)], buffers.at[d, 3], sems.at[parts + d]
                ).start()

    stores = []
    for d in list(range(1, parts)) + [0]:
        loads[d].wait()
        pltpu.make_async_copy(
            below.at[:, columns(d)], buffers.at[d, 3], sems.at[parts + d]
        ).wait()
        stores.append(pltpu.make_async_copy(buffers.at[d], pieces[d], sems.at[2 * parts + d]))
        stores[-1].start()
    for store in stores:
        store.wait()


def pack(parts, clip, plan, qkv, cot, below, above):
    rows, features = below.shape
    piece = jax.ShapeDtypeStruct((4, rows, features // parts), qkv.dtype)
    return pl.pallas_call(
        functools.partial(pack_kernel, parts, clip),
        out_shape=[piece] * parts,
        in_specs=[pl.BlockSpec(memory_space=SMEM)] + [pl.BlockSpec(memory_space=pl.ANY)] * 4,
        out_specs=[pl.BlockSpec(memory_space=pl.ANY)] * parts,
        scratch_shapes=[
            pltpu.VMEM((parts,) + piece.shape, piece.dtype),
            pltpu.SemaphoreType.DMA((3 * parts,)),
        ],
    )(plan, qkv, cot, below, above)


def assemble_kernel(parts, clip, plan, *refs):
    outs, grads, buffers, sems = refs[-4:]
    slot = plan[SLOT + clip]
    me = lax.axis_index("seq")
    if not parts:
        buffers[...] = jnp.zeros_like(buffers)
        targets = [outs.at[slot]] + [grads.at[i, slot] for i in range(3)]
        stores = [
            pltpu.make_async_copy(buffers, target, sems.at[i]) for i, target in enumerate(targets)
        ]
        for store in stores:
            store.start()
        for store in stores:
            store.wait()
        return
    width = refs[0].shape[2]
    triples = []
    for d in range(parts):
        columns = pl.ds(pl.multiple_of(lax.rem(me + d, parts) * width, HEAD), width)
        triples.append((refs[d].at[0], buffers.at[d, 0], outs.at[slot, :, columns]))
        rest = pl.ds(1, 3)
        triples.append((refs[d].at[rest], buffers.at[d, rest], grads.at[:, slot, :, columns]))
    relay(triples, sems)


def assemble(clip, plan, pieces, qkv, totals):
    parts = len(pieces)
    rows, features = qkv.shape[2:]
    any_space = pl.BlockSpec(memory_space=pl.ANY)
    operands = list(pieces) + list(totals)
    aliases = {1 + parts + i: i for i in range(len(totals))}
    return pl.pallas_call(
        functools.partial(assemble_kernel, parts, clip),
        out_shape=[
            jax.ShapeDtypeStruct(qkv.shape[1:], qkv.dtype),
            jax.ShapeDtypeStruct(qkv.shape, qkv.dtype),
        ],
        in_specs=[pl.BlockSpec(memory_space=SMEM)] + [any_space] * len(operands),
        out_specs=[any_space] * 2,
        scratch_shapes=[
            pltpu.VMEM(
                (parts,) + pieces[0].shape if parts else (rows, features), qkv.dtype
            ),
            pltpu.SemaphoreType.DMA((max(4 * parts, 4),)),
        ],
        input_output_aliases=aliases,
    )(plan, *operands)


def attention_kernel(parts, plan_ref, *refs):
    ins, outs = refs[:parts], refs[parts:]
    rows = ins[0].shape[1]
    extent = parts * rows
    count = plan_ref[parts]
    row_iota = lax.broadcasted_iota(jnp.int32, (rows, 1), 0)
    inside = jnp.concatenate([row_iota + plan_ref[d] < count for d in range(parts)], axis=0)

    def load(which):
        return jnp.concatenate([r[which] for r in ins], axis=0)

    q, k, v, g = load(0), load(1), load(2), load(3)
    g = jnp.where(inside, g, jnp.zeros((), g.dtype))
    nt = (((1,), (1,)), ((), ()))
    tn = (((0,), (0,)), ((), ()))
    nn = (((1,), (0,)), ((), ()))
    dot = functools.partial(lax.dot_general, preferred_element_type=jnp.float32)
    grad_k = grad_v = None
    out_rows, grad_q_rows = [], []
    step = min(256, extent)
    for start in range(0, extent, step):
        stop = min(start + step, extent)
        q_i, g_i = q[start:stop], g[start:stop]
        scores = jnp.where(inside, dot(k, q_i, nt), NEGATIVE)
        largest = jnp.max(scores, axis=0, keepdims=True)
        exponent = jnp.exp2((scores - largest) * (FACTOR * LOG2E))
        weights = exponent * (1.0 / jnp.sum(exponent, axis=0, keepdims=True))
        rounded = weights.astype(jnp.bfloat16)
        grad_weights = dot(v, g_i, nt)
        inner = jnp.sum(grad_weights * weights, axis=0, keepdims=True)
        score_grad = (weights * (grad_weights - inner)).astype(jnp.bfloat16)
        out_rows.append(dot(v, rounded, tn).T)
        grad_q_rows.append(dot(k, score_grad, tn).T)
        add_k = dot(score_grad, q_i, nn)
        add_v = dot(rounded, g_i, nn)
        grad_k = add_k if grad_k is None else grad_k + add_k
        grad_v = add_v if grad_v is None else grad_v + add_v
    out = jnp.where(inside, jnp.concatenate(out_rows, axis=0), 0.0).astype(jnp.bfloat16)
    grad_q = (jnp.concatenate(grad_q_rows, axis=0) * FACTOR).astype(jnp.bfloat16)
    grad_k = (grad_k * FACTOR).astype(jnp.bfloat16)
    grad_v = grad_v.astype(jnp.bfloat16)
    for d, ref in enumerate(outs):
        span = slice(d * rows, (d + 1) * rows)
        ref[0] = out[span]
        ref[1] = grad_q[span]
        ref[2] = grad_k[span]
        ref[3] = grad_v[span]


def attention(pieces, plan):
    parts = len(pieces)
    fields, rows, width = pieces[0].shape
    spec = pl.BlockSpec((fields, rows, HEAD), lambda h, plan: (0, 0, h))
    return pl.pallas_call(
        functools.partial(attention_kernel, parts),
        out_shape=[jax.ShapeDtypeStruct(p.shape, p.dtype) for p in pieces],
        grid_spec=pltpu.PrefetchScalarGridSpec(
            num_scalar_prefetch=1,
            grid=(width // HEAD,),
            in_specs=[spec] * parts,
            out_specs=[spec] * parts,
        ),
        compiler_params=pltpu.CompilerParams(vmem_limit_bytes=40 * 2**20),
        cost_estimate=pl.CostEstimate(
            flops=12 * (parts * rows) ** 2 * width,
            bytes_accessed=16 * parts * rows * width,
            transcendentals=(parts * rows) ** 2 * (width // HEAD),
        ),
    )(plan, *pieces)


def rotate(parts, block, distance):
    return lax.ppermute(block, "seq", [(i, (i + distance) % parts) for i in range(parts)])


def pair_runner(shares):
    def run(plan, qkv, cot, below, above):
        rows = below.shape[0]
        me = lax.axis_index("seq")
        arrived = []
        for clip, parts in enumerate(shares):
            if parts:
                pieces = pack(parts, clip, plan, qkv, cot, below, above)
                arrived.append(
                    [pieces[0]] + [rotate(parts, pieces[d], d) for d in range(1, parts)]
                )
            else:
                arrived.append([])
        returned = []
        for clip, parts in enumerate(shares):
            if not parts:
                returned.append([])
                continue
            starts = [
                jnp.where(me < parts, lax.rem(me - d + 2 * parts, parts), parts) * rows
                for d in range(parts)
            ]
            table = jnp.stack(starts + [plan[COUNT + clip]]).astype(jnp.int32)
            results = attention(arrived[clip], table)
            returned.append(
                [results[0]] + [rotate(parts, results[d], parts - d) for d in range(1, parts)]
            )
        totals = ()
        for clip in range(2):
            totals = assemble(clip, plan, returned[clip], qkv, totals)
        return tuple(totals)

    return run


def on_device(qkv, cotangent, lengths, target_group, target_slot):
    packed, cot = qkv[:, 0], cotangent[0]
    choices = extents(lax.axis_size("seq"), packed.shape[-1] // HEAD)
    tables = jnp.stack([lengths, target_group, target_slot])
    plan, up, down = make_plan(choices, tables, cot)
    below, above = shift_dp(up, 1), shift_dp(down, -1)
    classes = [0] + choices
    branches = [pair_runner((a, b)) for i, a in enumerate(classes) for b in classes[: i + 1]]
    outs, grads = lax.switch(plan[BRANCH], branches, plan, packed, cot, below, above)
    up, down = pick_outputs(plan, outs)
    attended = place_outputs(plan, outs, shift_dp(up, 1), shift_dp(down, -1))
    return attended[None], grads[:, None]


def solution(mesh):
    in_specs = (P(None, "dp", None, "seq", None), P("dp", None, "seq", None), P(), P(), P())
    out_specs = (P("dp", None, "seq", None), P(None, "dp", None, "seq", None))
    return jax.shard_map(
        on_device, mesh=mesh, in_specs=in_specs, out_specs=out_specs, check_vma=False
    )
```
